256 devices in a mesh: lon: 32 (over x, y, z_lo), lat: 8 (over z_hi, core).
Axes of the slice: x: 4, y: 4, z: 8 (z_hi: 4, z_lo: 2; z = z_hi * 2 + z_lo), core: 2. Of those that a mesh axis runs over, the one named last changes fastest.
Arguments:
- thermal_field: float32 [128, 16, 16384], P(None, 'lat', 'lon'), may hold values from -6 to 6
- zonal_weights: float32 [2, 16, 16384], P(None, 'lat', 'lon'), may hold values from 0.05 to 0.3
- meridional_weights: float32 [2, 16, 16384], P(None, 'lat', 'lon'), may hold values from 0.02 to 0.1
- gas_burden: bfloat16 [16, 16384, 2048], P('lat', 'lon'), may hold values from 0.5 to 2
- tier_air_weight: bfloat16 [16, 16384, 128], P('lat', 'lon'), may hold values from 0.5 to 2
- solar_elevation_factor: bfloat16 [16, 16384], P('lat', 'lon'), may hold values from 0.099609375 to 1
- ground_reflectance: bfloat16 [16, 16384], P('lat', 'lon'), may hold values from 0.049804688 to 0.8984375
- extinction_table: float32 [16, 224], replicated, may hold values from 2e-05 to 0.004
- incoming_irradiance: float32 [224], replicated, may hold values from 0.1 to 3
- daytime_tile_tally: int32 [8, 32], P('lat', 'lon'), may hold values from 1 to 256, 4096 in all within a row
- daytime_tile_order: int32 [8, 32, 256], P('lat', 'lon'), may hold values from 0 to 255, each once within a row
Outputs:
- temperature_next: float32 [128, 16, 16384], P(None, 'lat', 'lon')
The draws below stay inside these ranges and needn't reach their ends.
Inputs may be any that keep to these rules, and one draw needn't show every extreme that they name: `daytime_tile_tally`: in each latitude band the counts of the 32 devices sum to 4096, and some device of the band has all 256 blocks daylit. `daytime_tile_order`: each device's list names each of its 256 blocks once.
All inputs are finite; a program needn't handle non-finite values.
Results may differ from the reference program's by a relative error of at most 0.0006.
Values may be sent and summed in bfloat16 or wider, within the bound.
No kernel may reach another device: no remote copies, remote signals or barrier semaphores. Data moves between devices by JAX's collectives and lax.ppermute only.
A program may use at most 128 MiB of HBM per device.

```python
import math
import jax
import jax.numpy as jnp
import numpy as np
from jax import lax

VERTICAL_TIERS = 128
NG = 16
GPT = 224
BC = 4
DSTEPS = 2
LATC = 2
LONC = 512
NBLK = 256
MERIDIAN_POINTS = 16
ZONAL_POINTS = 16384
N_LON = 32
N_LAT = 8


def level_of(own_key, dims, split, least, top_value):
    gain, own = 1.0, jax.random.fold_in(own_key, 6)
    for axis_at, parts in split:
        heights = jnp.exp(jax.random.uniform(jax.random.fold_in(own, axis_at), (parts,), jnp.float32, least / len(split), top_value / len(split)))
        gain = gain * jnp.repeat(heights, dims[axis_at] // parts).reshape([-1 if axis == axis_at else 1 for axis in range(len(dims))])
    return gain


def length_profile(count, total, most, slope):
    portions = [(1 << 20) // math.isqrt(standing ** slope) + 1 for standing in range(2, count + 1)]
    spare, holding = total - most - (count - 1), [1] * (count - 1)
    while spare > 0:
        candidates = [i for i in range(count - 1) if holding[i] < most]
        mass, remaining = sum([portions[i] for i in candidates]), spare
        for i in candidates:
            extra = min(most - holding[i], max(1, remaining * portions[i] // mass), spare)
            holding[i] = holding[i] + extra
            spare = spare - extra
    return np.array([most] + holding)


def uneven_parts(stream_key, number_of, total, reach, slope):
    if number_of == 2:
        one = jax.random.randint(stream_key, (), max(1, total - reach), min(reach, total - 1) + 1)
        return jnp.stack([one, total - one])
    sizes = jnp.asarray(length_profile(number_of, total, reach, slope), jnp.int32)
    couples = (number_of - 1) // 2
    giver, sink = sizes[1:1 + 2 * couples:2], sizes[2:2 + 2 * couples:2]
    slack = jnp.minimum(giver - 1, reach - sink)
    passed = jax.random.randint(jax.random.fold_in(stream_key, 1), (couples,), 0, 1 << 20) % (slack + 1)
    sizes = sizes.at[1:1 + 2 * couples:2].set(giver - passed).at[2:2 + 2 * couples:2].set(sink + passed)
    return sizes[jax.random.permutation(jax.random.fold_in(stream_key, 2), number_of)]


def gaussian(rng, shape, scale, reach, split=(), kind=jnp.bfloat16):
    loudness = level_of(rng, shape, split, -0.22, 0.18) if split else 1.0
    entries = jax.random.normal(rng, shape, jnp.float32) * scale * loudness
    return jnp.minimum(jnp.maximum(entries, -reach), reach).astype(kind)


def setup_inputs(seed: int = 0) -> dict:
    arg_keys = jax.random.split(jax.random.key(seed), 12)
    return {
        "thermal_field": gaussian(arg_keys[0], (VERTICAL_TIERS, MERIDIAN_POINTS, ZONAL_POINTS), 1.0, 6.0, ((1, 8), (2, 32)), jnp.float32),
        "zonal_weights": jnp.clip(jnp.exp(math.log(0.3) - 1.7917595 * jax.random.uniform(arg_keys[1], (2, MERIDIAN_POINTS, ZONAL_POINTS), jnp.float32) ** level_of(arg_keys[1], (2, MERIDIAN_POINTS, ZONAL_POINTS), ((1, 8), (2, 32)), -0.2, 0.2)), 0.05, 0.3),
        "meridional_weights": jnp.clip(jnp.exp(math.log(0.1) - 1.609438 * jax.random.uniform(arg_keys[2], (2, MERIDIAN_POINTS, ZONAL_POINTS), jnp.float32) ** level_of(arg_keys[2], (2, MERIDIAN_POINTS, ZONAL_POINTS), ((1, 8), (2, 32)), -0.2, 0.2)), 0.02, 0.1),
        "gas_burden": jnp.clip(jnp.exp(math.log(2.0) - 1.3862944 * jax.random.uniform(arg_keys[3], (MERIDIAN_POINTS, ZONAL_POINTS, VERTICAL_TIERS * NG), jnp.float32) ** level_of(arg_keys[3], (MERIDIAN_POINTS, ZONAL_POINTS, VERTICAL_TIERS * NG), ((0, 8), (1, 32)), -0.2, 0.2)), 0.5, 2.0).astype(jnp.bfloat16),
        "tier_air_weight": jnp.clip(jnp.exp(math.log(2.0) - 1.3862944 * jax.random.uniform(arg_keys[4], (MERIDIAN_POINTS, ZONAL_POINTS, VERTICAL_TIERS), jnp.float32) ** level_of(arg_keys[4], (MERIDIAN_POINTS, ZONAL_POINTS, VERTICAL_TIERS), ((0, 8), (1, 32)), -0.2, 0.2)), 0.5, 2.0).astype(jnp.bfloat16),
        "solar_elevation_factor": jnp.clip(jnp.exp(math.log(1.0) - 2.306499 * jax.random.uniform(arg_keys[5], (MERIDIAN_POINTS, ZONAL_POINTS), jnp.float32) ** level_of(arg_keys[5], (MERIDIAN_POINTS, ZONAL_POINTS), ((0, 8), (1, 32)), -0.2, 0.2)), 0.099609375, 1.0).astype(jnp.bfloat16),
        "ground_reflectance": jnp.clip(0.049804688 + 0.8486328 * jax.random.uniform(arg_keys[6], (MERIDIAN_POINTS, ZONAL_POINTS), jnp.float32) ** level_of(arg_keys[6], (MERIDIAN_POINTS, ZONAL_POINTS), ((0, 8), (1, 32)), -0.2, 0.2), 0.049804688, 0.8984375).astype(jnp.bfloat16),
        "extinction_table": jnp.clip(jnp.exp(jax.random.uniform(arg_keys[7], (NG, GPT), jnp.float32, math.log(1.9999999494757503e-05), math.log(0.004))), 1.9999999494757503e-05, 0.004),
        "incoming_irradiance": jnp.clip(jnp.exp(jax.random.uniform(arg_keys[8], (GPT,), jnp.float32, math.log(0.1), math.log(3.0))), 0.1, 3.0),
        "daytime_tile_tally": jax.vmap(lambda own: uneven_parts(own, N_LON, N_LON * NBLK // 2, NBLK, 2))(jax.random.split(arg_keys[9], N_LAT)).reshape((N_LAT, N_LON)).astype(jnp.int32),
        "daytime_tile_order": jax.vmap(lambda own: jax.random.permutation(own, NBLK))(jax.random.split(arg_keys[10], N_LAT * N_LON)).reshape((N_LAT, N_LON, NBLK)).astype(jnp.int32),
    }


DIFFUSE = 1.66


def column_heating(gas_burden, tier_air_weight, solar_elevation_factor, ground_reflectance, extinction_table, incoming_irradiance):
    columns = gas_burden.shape[0]
    amounts = gas_burden.astype(jnp.float32).reshape(columns, VERTICAL_TIERS, NG)
    summed = jnp.cumsum(amounts, axis=1)
    column_above = jnp.concatenate([jnp.zeros((columns, 1, NG), jnp.float32), summed], axis=1)
    optical_depth = jnp.einsum("cij,jg->cig", column_above, extinction_table, precision=lax.Precision.HIGHEST)
    cosine_col = solar_elevation_factor.astype(jnp.float32)[:, None, None]
    downward = incoming_irradiance[None, None, :] * cosine_col * jnp.exp(-optical_depth / cosine_col)
    upward = ground_reflectance.astype(jnp.float32)[:, None, None] * downward[:, -1:, :] * jnp.exp(-DIFFUSE * (optical_depth[:, -1:, :] - optical_depth))
    net_flux = jnp.sum(downward - upward, axis=2)
    return (net_flux[:, :-1] - net_flux[:, 1:]) / tier_air_weight.astype(jnp.float32)


def reference(thermal_field, zonal_weights, meridional_weights, gas_burden, tier_air_weight, solar_elevation_factor, ground_reflectance, extinction_table, incoming_irradiance, daytime_tile_tally, daytime_tile_order):
    prognostic_field = thermal_field
    for step_index in range(DSTEPS):
        western = jnp.roll(prognostic_field, 1, axis=2)
        eastern = jnp.roll(prognostic_field, -1, axis=2)
        padded = jnp.pad(prognostic_field, ((0, 0), (1, 1), (0, 0)))
        southern = padded[:, :-2, :]
        northern = padded[:, 2:, :]
        prognostic_field = prognostic_field + zonal_weights[0] * (western - prognostic_field) + zonal_weights[1] * (eastern - prognostic_field) + meridional_weights[0] * (southern - prognostic_field) + meridional_weights[1] * (northern - prognostic_field)
    lat_cells, zonal_point_number = solar_elevation_factor.shape
    groups = lat_cells * zonal_point_number // LONC

    def one_group(pieces):
        return column_heating(pieces[0], pieces[1], pieces[2], pieces[3], extinction_table, incoming_irradiance)

    heating = lax.map(one_group, (gas_burden.reshape(groups, LONC, VERTICAL_TIERS * NG), tier_air_weight.reshape(groups, LONC, VERTICAL_TIERS), solar_elevation_factor.reshape(groups, LONC), ground_reflectance.reshape(groups, LONC)))
    heating = heating.reshape(lat_cells, zonal_point_number, VERTICAL_TIERS)
    position = jnp.arange(NBLK, dtype=jnp.int32)
    live_rank = position[None, None, :, None] < daytime_tile_tally[:, :, None, None]
    named = daytime_tile_order[:, :, :, None] == position[None, None, None, :]
    lit_flags = jnp.sum(jnp.where(live_rank & named, 1.0, 0.0), axis=2).astype(jnp.float32)
    lit_flags = lit_flags.reshape(N_LAT, N_LON, LATC, LONC // BC)
    lit_flags = jnp.repeat(lit_flags, BC, axis=3).transpose(0, 2, 1, 3).reshape(lat_cells, zonal_point_number)
    heating = heating * lit_flags[:, :, None]
    return prognostic_field + heating.transpose(2, 0, 1)
```

```python
import functools
import math

import jax
import jax.numpy as jnp
from jax import lax
from jax.experimental import pallas as pl
from jax.experimental.pallas import tpu as pltpu
from jax.sharding import PartitionSpec as P

DSTEPS = 2
DIFFUSE = 1.66
LOG2E = math.log2(math.e)
TIERS, TERMS, POINTS, BLOCK = 128, 16, 224, 4
RUN = 8
RUNS = TIERS // RUN
TILE = 256
ROWS = 8
LANES = 128


def across(row, rows):
    return jnp.broadcast_to(row, (rows, row.shape[1]))


def halves(values):
    high = values.astype(jnp.bfloat16)
    low = (values - high.astype(jnp.float32)).astype(jnp.bfloat16)
    return jnp.concatenate([high, low], axis=1)


def thirds(values):
    high = values.astype(jnp.bfloat16)
    left = values - high.astype(jnp.float32)
    middle = left.astype(jnp.bfloat16)
    low = (left - middle.astype(jnp.float32)).astype(jnp.bfloat16)
    return high, middle, low


def by_rows(left, right):
    return lax.dot_general(left, right, (((1,), (1,)), ((), ())), preferred_element_type=jnp.float32)


def rad_kernel(rows, tally_ref, gas_ref, mass_ref, cos_ref, alb_ref, order_ref, table_ref, light_ref, out_ref,
               lhs_ref, slope_ref, down_ref, up_ref, weight_ref, part_a, part_b, net_ref):
    width = 2 * TILE
    tiles = len(rows) * 2
    table = table_ref[...] * DIFFUSE
    table = jnp.concatenate([table, jnp.zeros((TERMS, 256 - POINTS), jnp.float32)], axis=1)
    stacked = jnp.concatenate([table] * RUN, axis=0).T[:POINTS]
    whole = halves(stacked * LOG2E)
    term = lax.broadcasted_iota(jnp.int32, (POINTS, 2 * LANES), 1) % LANES // TERMS
    for r in range(1, RUN + 1):
        chosen = jnp.where(term < r, whole.astype(jnp.float32), 0.0)
        lhs_ref[(r - 1) * POINTS:r * POINTS, :] = chosen.astype(jnp.bfloat16)
    light = jnp.concatenate([light_ref[...], jnp.ones((1, 256 - POINTS), jnp.float32)], axis=1)
    light = across(jnp.log(light) * LOG2E, LANES).T[:POINTS]
    light = jnp.concatenate([light, light], axis=1)
    eye = (lax.broadcasted_iota(jnp.int32, (LANES, LANES), 0)
           == lax.broadcasted_iota(jnp.int32, (LANES, LANES), 1)).astype(jnp.float32).astype(jnp.bfloat16)
    listed = across(order_ref[...].astype(jnp.float32), LANES).T
    rank = lax.broadcasted_iota(jnp.int32, listed.shape, 0)
    listed = jnp.where(rank < tally_ref[0, 0], listed, -1.0)

    for n in range(tiles):
        row, first = rows[n // 2], (n % 2) * TILE
        cols = slice(first, first + TILE)
        cosine = cos_ref[row:row + 1, cols].astype(jnp.float32)
        albedo = alb_ref[row:row + 1, cols].astype(jnp.float32)
        slope = -1.0 / (DIFFUSE * cosine)
        slope_ref[n] = across(slope, ROWS)
        amount = gas_ref[n // 2, cols, 0:LANES].astype(jnp.float32)
        for b in range(1, RUNS):
            amount = amount + gas_ref[n // 2, cols, b * LANES:(b + 1) * LANES].astype(jnp.float32)
        total = None
        for piece in thirds(amount):
            got = by_rows(whole, jnp.concatenate([piece, piece], axis=1))
            total = got if total is None else total + got
        floor = light + (jnp.log(albedo) * LOG2E) + (slope - 1.0) * total
        down_ref[n] = light
        up_ref[n] = floor
        top = jnp.exp2(light) - jnp.exp2(floor)
        net_ref[n] = jnp.sum(top.reshape(POINTS // ROWS, ROWS, TILE), axis=0)
        mass = by_rows(eye, mass_ref[n // 2, cols, :])
        lit = []
        for t in range(TILE // LANES):
            block = (lax.broadcasted_iota(jnp.int32, listed.shape, 1) + (row * width + first + t * LANES)) // BLOCK
            hit = jnp.where(listed == block.astype(jnp.float32), 1.0, 0.0)
            lit.append(jnp.sum(hit, axis=0, keepdims=True))
        lit = jnp.concatenate(lit, axis=1)
        weight_ref[n] = cosine * lit / mass

    def parts(n):
        tile, b = n // RUNS, n % RUNS
        g = gas_ref[tile // 2, pl.ds(pl.multiple_of(tile % 2 * TILE, TILE), TILE),
                    pl.ds(pl.multiple_of(b * LANES, LANES), LANES)]
        return by_rows(lhs_ref[...], jnp.concatenate([g, g], axis=1))

    def process(part_ref, n):
        tile, b = n // RUNS, n % RUNS
        levels = pl.ds(pl.multiple_of(b * RUN, RUN), RUN)
        for t in range(TILE // LANES):
            cols = slice(t * LANES, (t + 1) * LANES)
            s = slope_ref[tile, :, cols]
            acc = [None] * (RUN + 1)
            for q in range(POINTS // ROWS):
                here = slice(q * ROWS, (q + 1) * ROWS)
                down0 = down_ref[tile, here, cols]
                up0 = up_ref[tile, here, cols]
                for r in range(1, RUN + 1):
                    at = (r - 1) * POINTS + q * ROWS
                    part = part_ref[at:at + ROWS, cols]
                    down = s * part + down0
                    up = part + up0
                    value = jnp.exp2(down) - jnp.exp2(up)
                    acc[r] = value if acc[r] is None else acc[r] + value
                down_ref[tile, here, cols] = down
                up_ref[tile, here, cols] = up
            acc[0] = net_ref[tile, :, cols]
            net_ref[tile, :, cols] = acc[RUN]
            diffs = []
            for r in range(1, RUN + 1):
                diffs.append(jnp.sum(acc[r - 1] - acc[r], axis=0, keepdims=True))
            place = pl.ds(pl.multiple_of(tile % 2 * TILE + t * LANES, LANES), LANES)
            out_ref[tile // 2, levels, place] = jnp.concatenate(diffs, axis=0) * weight_ref[tile, levels, cols]

    part_a[...] = parts(0)
    last = tiles * RUNS - 1

    def two_runs(h, carry):
        n = 2 * h
        part_b[...] = parts(n + 1)
        process(part_a, n)
        part_a[...] = parts(jnp.minimum(n + 2, last))
        process(part_b, n + 1)
        return carry

    lax.fori_loop(0, tiles * RUNS // 2, two_runs, 0)


def radiation(gas, mass, cosine, albedo, order, table, light, tally, rows=(0, 1)):
    tiles = 2 * len(rows)
    whole = lambda shape: pl.BlockSpec(shape, lambda: (0,) * len(shape))
    n = len(rows)
    return pl.pallas_call(
        functools.partial(rad_kernel, rows),
        out_shape=jax.ShapeDtypeStruct((n, TIERS, 512), jnp.float32),
        in_specs=[
            pl.BlockSpec(memory_space=pltpu.SMEM),
            pl.BlockSpec((n, 512, TIERS * TERMS), lambda: (rows[0] // n, 0, 0)),
            pl.BlockSpec((n, 512, TIERS), lambda: (rows[0] // n, 0, 0)),
            whole((2, 512)), whole((2, 512)), whole((1, 256)), whole((TERMS, POINTS)), whole((1, POINTS)),
        ],
        out_specs=whole((n, TIERS, 512)),
        scratch_shapes=[
            pltpu.VMEM((RUN * POINTS, 2 * LANES), jnp.bfloat16),
            pltpu.VMEM((tiles, ROWS, TILE), jnp.float32),
            pltpu.VMEM((tiles, POINTS, TILE), jnp.float32),
            pltpu.VMEM((tiles, POINTS, TILE), jnp.float32),
            pltpu.VMEM((tiles, TIERS, TILE), jnp.float32),
            pltpu.VMEM((RUN * POINTS, TILE), jnp.float32),
            pltpu.VMEM((RUN * POINTS, TILE), jnp.float32),
            pltpu.VMEM((tiles, ROWS, TILE), jnp.float32),
        ],
        compiler_params=pltpu.CompilerParams(vmem_limit_bytes=40 * 1024 * 1024),
    )(tally, gas, mass, cosine, albedo, order, table, light)

def padded(cells, sides, width, closed):
    for axis, dim in sides:
        count = lax.axis_size(axis)
        ends = count if closed else count - 1
        head = lax.slice_in_dim(cells, 0, width, axis=dim)
        tail = lax.slice_in_dim(cells, cells.shape[dim] - width, cells.shape[dim], axis=dim)
        cells = jnp.concatenate(
            [
                lax.ppermute(tail, axis, [(i, (i + 1) % count) for i in range(ends)]),
                cells,
                lax.ppermute(head, axis, [((i + 1) % count, i) for i in range(ends)]),
            ],
            axis=dim,
        )
    return cells


def march_forward(thermal_field, zonal_weights, meridional_weights):
    prognostic_field = thermal_field
    for step_index in range(DSTEPS):
        lon_rims = padded(prognostic_field, (("lon", 2),), 1, True)
        lat_rims = padded(prognostic_field.astype(jnp.bfloat16), (("lat", 1),), 1, False).astype(
            prognostic_field.dtype
        )
        western = lon_rims[:, :, :-2]
        eastern = lon_rims[:, :, 2:]
        southern = lat_rims[:, :-2, :]
        northern = lat_rims[:, 2:, :]
        prognostic_field = (
            prognostic_field
            + zonal_weights[0] * (western - prognostic_field)
            + zonal_weights[1] * (eastern - prognostic_field)
            + meridional_weights[0] * (southern - prognostic_field)
            + meridional_weights[1] * (northern - prognostic_field)
        )
    return prognostic_field


def per_device(
    thermal_field,
    zonal_weights,
    meridional_weights,
    gas_burden,
    tier_air_weight,
    solar_elevation_factor,
    ground_reflectance,
    extinction_table,
    incoming_irradiance,
    daytime_tile_tally,
    daytime_tile_order,
):
    prognostic_field = march_forward(thermal_field, zonal_weights, meridional_weights)
    heat = radiation(
        gas_burden,
        tier_air_weight,
        solar_elevation_factor,
        ground_reflectance,
        daytime_tile_order.reshape(1, -1),
        extinction_table,
        incoming_irradiance.reshape(1, -1),
        daytime_tile_tally,
    )
    return prognostic_field + heat.transpose(1, 0, 2)


def solution(mesh):
    placed = (
        P(None, "lat", "lon"),
        P(None, "lat", "lon"),
        P(None, "lat", "lon"),
        P("lat", "lon", None),
        P("lat", "lon", None),
        P("lat", "lon"),
        P("lat", "lon"),
        P(),
        P(),
        P("lat", "lon"),
        P("lat", "lon", None),
    )
    return jax.shard_map(
        per_device, mesh=mesh, in_specs=placed, out_specs=P(None, "lat", "lon"), check_vma=False
    )
```

```python
import functools
import math

import jax
import jax.numpy as jnp
from jax import lax
from jax.experimental import pallas as pl
from jax.experimental.pallas import tpu as pltpu
from jax.sharding import PartitionSpec as P

DSTEPS = 2
DIFFUSE = 1.66
LOG2E = math.log2(math.e)
TIERS, TERMS, POINTS, BLOCK = 128, 16, 224, 4
RUN = 8
RUNS = TIERS // RUN
TILE = 256
ROWS = 8
LANES = 128
TOGETHER = 4
HALO = 128
VMEM_BYTES = 60 * 1024 * 1024


def across(row, rows):
    return jnp.broadcast_to(row, (rows, row.shape[1]))


def halves(values):
    high = values.astype(jnp.bfloat16)
    low = (values - high.astype(jnp.float32)).astype(jnp.bfloat16)
    return jnp.concatenate([high, low], axis=1)


def thirds(values):
    high = values.astype(jnp.bfloat16)
    left = values - high.astype(jnp.float32)
    middle = left.astype(jnp.bfloat16)
    low = (left - middle.astype(jnp.float32)).astype(jnp.bfloat16)
    return high, middle, low


def by_rows(left, right):
    return lax.dot_general(left, right, (((1,), (1,)), ((), ())), preferred_element_type=jnp.float32)


def rad_kernel(rows, tally_ref, gas_hbm, mass_hbm, cos_ref, alb_ref, order_ref, table_ref, light_ref, out_ref,
               lhs_ref, slope_ref, down_ref, up_ref, weight_ref, part_a, part_b, net_ref,
               gas_ref, mass_ref, gas_sem, mass_sem):
    width = 2 * TILE
    tiles = len(rows) * 2
    gas_copies, mass_copies = [], []
    for n in range(tiles):
        cols = slice(n % 2 * TILE, (n % 2 + 1) * TILE)
        gas_copies.append(pltpu.make_async_copy(
            gas_hbm.at[rows[n // 2], cols], gas_ref.at[n // 2, cols], gas_sem.at[n]))
        mass_copies.append(pltpu.make_async_copy(
            mass_hbm.at[rows[n // 2], cols], mass_ref.at[n // 2, cols], mass_sem.at[n]))
    for copy in gas_copies + mass_copies:
        copy.start()
    table = table_ref[...] * DIFFUSE
    table = jnp.concatenate([table, jnp.zeros((TERMS, 256 - POINTS), jnp.float32)], axis=1)
    stacked = jnp.concatenate([table] * RUN, axis=0).T[:POINTS]
    whole = halves(stacked * LOG2E)
    term = lax.broadcasted_iota(jnp.int32, (POINTS, 2 * LANES), 1) % LANES // TERMS
    for r in range(1, RUN + 1):
        chosen = jnp.where(term < r, whole.astype(jnp.float32), 0.0)
        lhs_ref[(r - 1) * POINTS:r * POINTS, :] = chosen.astype(jnp.bfloat16)
    light = jnp.concatenate([light_ref[...], jnp.ones((1, 256 - POINTS), jnp.float32)], axis=1)
    light = across(jnp.log(light) * LOG2E, LANES).T[:POINTS]
    light = jnp.concatenate([light, light], axis=1)
    eye = (lax.broadcasted_iota(jnp.int32, (LANES, LANES), 0)
           == lax.broadcasted_iota(jnp.int32, (LANES, LANES), 1)).astype(jnp.float32).astype(jnp.bfloat16)
    listed = across(order_ref[...].astype(jnp.float32), LANES).T
    rank = lax.broadcasted_iota(jnp.int32, listed.shape, 0)
    listed = jnp.where(rank < tally_ref[0, 0], listed, -1.0)

    for n in range(tiles):
        row, first = rows[n // 2], (n % 2) * TILE
        cols = slice(first, first + TILE)
        cosine = cos_ref[row:row + 1, cols].astype(jnp.float32)
        albedo = alb_ref[row:row + 1, cols].astype(jnp.float32)
        slope = -1.0 / (DIFFUSE * cosine)
        slope_ref[n] = across(slope, ROWS)
        gas_copies[n].wait()
        mass_copies[n].wait()
        amount = gas_ref[n // 2, cols, 0:LANES].astype(jnp.float32)
        for b in range(1, RUNS):
            amount = amount + gas_ref[n // 2, cols, b * LANES:(b + 1) * LANES].astype(jnp.float32)
        total = None
        for piece in thirds(amount):
            got = by_rows(whole, jnp.concatenate([piece, piece], axis=1))
            total = got if total is None else total + got
        floor = light + (jnp.log(albedo) * LOG2E) + (slope - 1.0) * total
        down_ref[n] = light
        up_ref[n] = floor
        top = jnp.exp2(light) - jnp.exp2(floor)
        net_ref[n] = jnp.sum(top.reshape(POINTS // ROWS, ROWS, TILE), axis=0)
        mass = by_rows(eye, mass_ref[n // 2, cols, :])
        lit = []
        for t in range(TILE // LANES):
            block = (lax.broadcasted_iota(jnp.int32, listed.shape, 1) + (row * width + first + t * LANES)) // BLOCK
            hit = jnp.where(listed == block.astype(jnp.float32), 1.0, 0.0)
            lit.append(jnp.sum(hit, axis=0, keepdims=True))
        lit = jnp.concatenate(lit, axis=1)
        weight_ref[n] = cosine * lit / mass

    def parts(n):
        tile, b = n >> 4, n & (RUNS - 1)
        g = gas_ref[tile >> 1, pl.ds(pl.multiple_of((tile & 1) * TILE, TILE), TILE),
                    pl.ds(pl.multiple_of(b * LANES, LANES), LANES)]
        return by_rows(lhs_ref[...], jnp.concatenate([g, g], axis=1))

    def process(part_ref, n):
        tile, b = n >> 4, n & (RUNS - 1)
        levels = pl.ds(pl.multiple_of(b * RUN, RUN), RUN)
        for t in range(TILE // LANES):
            cols = slice(t * LANES, (t + 1) * LANES)
            s = slope_ref[tile, :, cols]
            acc = [None] * (RUN + 1)
            for q in range(POINTS // ROWS):
                here = slice(q * ROWS, (q + 1) * ROWS)
                down0 = down_ref[tile, here, cols]
                up0 = up_ref[tile, here, cols]
                for r in range(1, RUN + 1):
                    at = (r - 1) * POINTS + q * ROWS
                    part = part_ref[at:at + ROWS, cols]
                    down = s * part + down0
                    up = part + up0
                    light = jnp.exp2(down)
                    acc[r] = (light if acc[r] is None else acc[r] + light) - jnp.exp2(up)
                down_ref[tile, here, cols] = down
                up_ref[tile, here, cols] = up
            acc[0] = net_ref[tile, :, cols]
            net_ref[tile, :, cols] = acc[RUN]
            diffs = []
            for r in range(1, RUN + 1):
                diffs.append(jnp.sum(acc[r - 1] - acc[r], axis=0, keepdims=True))
            place = pl.ds(pl.multiple_of((tile & 1) * TILE + t * LANES, LANES), LANES)
            out_ref[tile >> 1, levels, place] = jnp.concatenate(diffs, axis=0) * weight_ref[tile, levels, cols]

    part_a[...] = parts(0)
    last = tiles * RUNS - 1

    def some_runs(h, carry):
        for u in range(TOGETHER):
            n = TOGETHER * h + u
            now, later = (part_a, part_b) if u % 2 == 0 else (part_b, part_a)
            later[...] = parts(jnp.minimum(n + 1, last))
            process(now, n)
        return carry

    lax.fori_loop(0, tiles * RUNS // TOGETHER, some_runs, 0)


def radiation(gas, mass, cosine, albedo, order, table, light, tally, rows=(0, 1)):
    tiles = 2 * len(rows)
    whole = lambda shape: pl.BlockSpec(shape, lambda: (0,) * len(shape))
    n = len(rows)
    return pl.pallas_call(
        functools.partial(rad_kernel, rows),
        out_shape=jax.ShapeDtypeStruct((n, TIERS, 512), jnp.float32),
        in_specs=[
            pl.BlockSpec(memory_space=pltpu.SMEM),
            pl.BlockSpec(memory_space=pl.ANY),
            pl.BlockSpec(memory_space=pl.ANY),
            whole((2, 512)), whole((2, 512)), whole((1, 256)), whole((TERMS, POINTS)), whole((1, POINTS)),
        ],
        out_specs=whole((n, TIERS, 512)),
        scratch_shapes=[
            pltpu.VMEM((RUN * POINTS, 2 * LANES), jnp.bfloat16),
            pltpu.VMEM((tiles, ROWS, TILE), jnp.float32),
            pltpu.VMEM((tiles, POINTS, TILE), jnp.float32),
            pltpu.VMEM((tiles, POINTS, TILE), jnp.float32),
            pltpu.VMEM((tiles, TIERS, TILE), jnp.float32),
            pltpu.VMEM((RUN * POINTS, TILE), jnp.float32),
            pltpu.VMEM((RUN * POINTS, TILE), jnp.float32),
            pltpu.VMEM((tiles, ROWS, TILE), jnp.float32),
            pltpu.VMEM((n, 512, TIERS * TERMS), jnp.bfloat16),
            pltpu.VMEM((n, 512, TIERS), jnp.bfloat16),
            pltpu.SemaphoreType.DMA((tiles,)),
            pltpu.SemaphoreType.DMA((tiles,)),
        ],
        compiler_params=pltpu.CompilerParams(vmem_limit_bytes=VMEM_BYTES),
        cost_estimate=pl.CostEstimate(
            flops=10 ** 10 * n, bytes_accessed=3 * 10 ** 6 * n, transcendentals=3 * 10 ** 7 * n
        ),
    )(tally, gas, mass, cosine, albedo, order, table, light)


def step(field, west, east, south, north, weights):
    return (
        field
        + weights[0] * (west - field)
        + weights[1] * (east - field)
        + weights[2] * (south - field)
        + weights[3] * (north - field)
    )


def march_kernel(own_ref, south_ref, north_ref, west_ref, east_ref, heat0_ref, heat1_ref, out_ref):
    width = own_ref.shape[2]
    rows = {-2: (south_ref, 0), -1: (south_ref, 1), 0: (own_ref, 0), 1: (own_ref, 1), 2: (north_ref, 0), 3: (north_ref, 1)}
    middle = slice(HALO, HALO + width)

    def plain(row, levels):
        ref, at = rows[row]
        return ref[levels, at, :]

    def wide(row, levels):
        return jnp.concatenate(
            [west_ref[levels, row + 1, :], plain(row, levels), east_ref[levels, row + 1, :]], axis=1
        )

    def west_of(cells):
        return pltpu.roll(cells, 1, 1)

    def east_of(cells):
        return pltpu.roll(cells, cells.shape[1] - 1, 1)

    weights = {}
    for row in (0, 1):
        weights[row] = [wide(row, slice(TIERS + k, TIERS + k + 1)) for k in range(4)]
    for row in (-1, 2):
        weights[row] = [plain(row, slice(TIERS + k, TIERS + k + 1)) for k in range(4)]
    chunk = 16

    def levels_step(h, carry):
        levels = pl.ds(pl.multiple_of(h * chunk, chunk), chunk)
        first = {row: wide(row, levels) for row in (-1, 0, 1, 2)}
        second = {}
        for row in (0, 1):
            f = first[row]
            second[row] = step(f, west_of(f), east_of(f), first[row - 1], first[row + 1], weights[row])
        for row in (-1, 2):
            f = first[row]
            south = plain(row - 1, levels) if row < 0 else first[row - 1][:, middle]
            north = first[row + 1][:, middle] if row < 0 else plain(row + 1, levels)
            second[row] = step(
                f[:, middle], west_of(f)[:, middle], east_of(f)[:, middle], south, north, weights[row]
            )
        for row, heat_ref in ((0, heat0_ref), (1, heat1_ref)):
            f = second[row]
            south = second[row - 1] if row == 0 else second[row - 1][:, middle]
            north = second[row + 1][:, middle] if row == 0 else second[row + 1]
            third = step(
                f[:, middle], west_of(f)[:, middle], east_of(f)[:, middle], south, north,
                [w[:, middle] for w in weights[row]],
            )
            out_ref[levels, row, :] = third + heat_ref[0, levels, :]
        return carry

    lax.fori_loop(0, TIERS // chunk, levels_step, 0)


def march(own, south, north, west, east, heat0, heat1):
    return pl.pallas_call(
        march_kernel,
        out_shape=jax.ShapeDtypeStruct((TIERS, own.shape[1], own.shape[2]), jnp.float32),
        compiler_params=pltpu.CompilerParams(vmem_limit_bytes=VMEM_BYTES),
    )(own, south, north, west, east, heat0, heat1)


def shifted(cells, axis, by, closed):
    count = lax.axis_size(axis)
    pairs = [(i, (i + by) % count) for i in range(count) if closed or 0 <= i + by < count]
    return lax.ppermute(cells, axis, pairs)


def per_device(
    thermal_field,
    zonal_weights,
    meridional_weights,
    gas_burden,
    tier_air_weight,
    solar_elevation_factor,
    ground_reflectance,
    extinction_table,
    incoming_irradiance,
    daytime_tile_tally,
    daytime_tile_order,
):
    def heating(row, gas):
        return radiation(
            gas,
            tier_air_weight,
            solar_elevation_factor,
            ground_reflectance,
            daytime_tile_order.reshape(1, -1),
            extinction_table,
            incoming_irradiance.reshape(1, -1),
            daytime_tile_tally,
            rows=(row,),
        )

    own = jnp.concatenate([thermal_field, zonal_weights, meridional_weights], axis=0)
    south = shifted(own, "lat", 1, False)
    north = shifted(own, "lat", -1, False)
    heat0 = heating(0, gas_burden)
    south, north, heat0 = lax.optimization_barrier((south, north, heat0))
    near = jnp.concatenate([south[:, 1:], own, north[:, :1]], axis=1)
    last, first = near[:, :, -HALO:], near[:, :, :HALO]
    gas_burden, last, first = lax.optimization_barrier((gas_burden, last, first))
    west = shifted(last, "lon", 1, True)
    east = shifted(first, "lon", -1, True)
    heat1 = heating(1, gas_burden)
    return march(own, south, north, west, east, heat0, heat1)


def solution(mesh):
    placed = (
        P(None, "lat", "lon"),
        P(None, "lat", "lon"),
        P(None, "lat", "lon"),
        P("lat", "lon", None),
        P("lat", "lon", None),
        P("lat", "lon"),
        P("lat", "lon"),
        P(),
        P(),
        P("lat", "lon"),
        P("lat", "lon", None),
    )
    return jax.shard_map(
        per_device, mesh=mesh, in_specs=placed, out_specs=P(None, "lat", "lon"), check_vma=False
    )
```

```python
import functools
import math

import jax
import jax.numpy as jnp
from jax import lax
from jax.experimental import pallas as pl
from jax.experimental.pallas import tpu as pltpu
from jax.sharding import PartitionSpec as P

DSTEPS = 2
DIFFUSE = 1.66
LOG2E = math.log2(math.e)
TIERS, TERMS, POINTS, BLOCK = 128, 16, 224, 4
RUN = 8
RUNS = TIERS // RUN
TILE = 256
ROWS = 8
LANES = 128
TOGETHER = 4
HALO = 128
ROWS_OF_LAT, HALVES = 2, 2
MIB = 1024 * 1024


def across(row, rows):
    return jnp.broadcast_to(row, (rows, row.shape[1]))


def halves(values):
    high = values.astype(jnp.bfloat16)
    low = (values - high.astype(jnp.float32)).astype(jnp.bfloat16)
    return jnp.concatenate([high, low], axis=1)


def thirds(values):
    high = values.astype(jnp.bfloat16)
    left = values - high.astype(jnp.float32)
    middle = left.astype(jnp.bfloat16)
    low = (left - middle.astype(jnp.float32)).astype(jnp.bfloat16)
    return high, middle, low


def by_rows(left, right):
    return lax.dot_general(left, right, (((1,), (1,)), ((), ())), preferred_element_type=jnp.float32)


def rad_kernel(tally_ref, gas_hbm, mass_hbm, cos_ref, alb_ref, order_ref, table_ref, light_ref, out_ref,
               lhs_ref, slope_ref, down_ref, up_ref, weight_ref, part_a, part_b, net_ref, whole_ref, light_log_ref, listed_ref,
               gas_ref, mass_ref, gas_sem, mass_sem):
    width = 2 * TILE

    def copies(row, half):
        cols = pl.ds(half * TILE, TILE)
        return (
            pltpu.make_async_copy(gas_hbm.at[row, cols], gas_ref.at[row, cols], gas_sem.at[row, half]),
            pltpu.make_async_copy(mass_hbm.at[row, cols], mass_ref.at[row, cols], mass_sem.at[row, half]),
        )

    for row in range(ROWS_OF_LAT):
        for half in range(HALVES):
            for copy in copies(row, half):
                copy.start()
    table = table_ref[...] * DIFFUSE
    table = jnp.concatenate([table, jnp.zeros((TERMS, 256 - POINTS), jnp.float32)], axis=1)
    stacked = jnp.concatenate([table] * RUN, axis=0).T[:POINTS]
    whole = halves(stacked * LOG2E)
    term = (lax.broadcasted_iota(jnp.int32, (1, 2 * LANES), 1) & (LANES - 1)) >> 4
    whole_wide = whole.astype(jnp.float32)
    for r in range(1, RUN + 1):
        chosen = jnp.where(term < r, whole_wide, 0.0)
        lhs_ref[(r - 1) * POINTS:r * POINTS, :] = chosen.astype(jnp.bfloat16)
    light = jnp.concatenate([light_ref[...], jnp.ones((1, 256 - POINTS), jnp.float32)], axis=1)
    light = across(jnp.log(light) * LOG2E, LANES).T[:POINTS]
    light_log_ref[...] = light
    whole_ref[...] = whole
    listed = across(order_ref[...].astype(jnp.float32), LANES).T
    rank = lax.broadcasted_iota(jnp.int32, listed.shape, 0)
    listed_ref[...] = jnp.where(rank < tally_ref[0, 0], listed, -1.0)

    def prepare(row, half):
        first = half * TILE
        cols = slice(first, first + TILE)

        def of_row(ref):
            both = ref[:, cols].astype(jnp.float32)
            return jnp.where(row == 0, both[0:1], both[1:2])

        cosine, albedo = of_row(cos_ref), of_row(alb_ref)
        slope = -1.0 / (DIFFUSE * cosine)
        slope_ref[half] = across(slope, ROWS)
        for copy in copies(row, half):
            copy.wait()
        amount = gas_ref[row, cols, 0:LANES].astype(jnp.float32)
        for b in range(1, RUNS):
            amount = amount + gas_ref[row, cols, b * LANES:(b + 1) * LANES].astype(jnp.float32)
        total = None
        for piece in thirds(amount):
            got = by_rows(whole_ref[...], jnp.concatenate([piece, piece], axis=1))
            total = got if total is None else total + got
        light = jnp.concatenate([light_log_ref[...]] * 2, axis=1)
        floor = light + (jnp.log(albedo) * LOG2E) + (slope - 1.0) * total
        down_ref[half] = light
        up_ref[half] = floor
        top = jnp.exp2(light) - jnp.exp2(floor)
        net_ref[half] = jnp.sum(top.reshape(POINTS // ROWS, ROWS, TILE), axis=0)
        eye = (lax.broadcasted_iota(jnp.int32, (LANES, LANES), 0)
               == lax.broadcasted_iota(jnp.int32, (LANES, LANES), 1)).astype(jnp.float32).astype(jnp.bfloat16)
        mass = by_rows(eye, mass_ref[row, cols, :])
        lit = []
        for t in range(TILE // LANES):
            block = (lax.broadcasted_iota(jnp.int32, (1, LANES), 1) + (row * width + first + t * LANES)) >> 2
            hit = jnp.where(listed_ref[...] == block.astype(jnp.float32), 1.0, 0.0)
            lit.append(jnp.sum(hit, axis=0, keepdims=True))
        lit = jnp.concatenate(lit, axis=1)
        weight_ref[half] = cosine * lit / mass

    def run_row(row, carry):
        for half in range(HALVES):
            prepare(row, half)

        def place(n):
            half, b = n >> 4, n & (RUNS - 1)
            return half, pl.multiple_of(half * TILE, TILE), b

        def parts(n):
            half, first, b = place(n)
            g = gas_ref[row, pl.ds(first, TILE), pl.ds(pl.multiple_of(b * LANES, LANES), LANES)]
            return by_rows(lhs_ref[...], jnp.concatenate([g, g], axis=1))

        def process(part_ref, n):
            half, first, b = place(n)
            levels = pl.ds(pl.multiple_of(b * RUN, RUN), RUN)
            for t in range(TILE // LANES):
                cols = slice(t * LANES, (t + 1) * LANES)
                s = slope_ref[half, :, cols]
                acc = [None] * (RUN + 1)
                for q in range(POINTS // ROWS):
                    here = slice(q * ROWS, (q + 1) * ROWS)
                    down0 = down_ref[half, here, cols]
                    up0 = up_ref[half, here, cols]
                    for r in range(1, RUN + 1):
                        at = (r - 1) * POINTS + q * ROWS
                        part = part_ref[at:at + ROWS, cols]
                        down = s * part + down0
                        up = part + up0
                        light = jnp.exp2(down)
                        acc[r] = (light if acc[r] is None else acc[r] + light) - jnp.exp2(up)
                    down_ref[half, here, cols] = down
                    up_ref[half, here, cols] = up
                acc[0] = net_ref[half, :, cols]
                net_ref[half, :, cols] = acc[RUN]
                diffs = []
                for r in range(1, RUN + 1):
                    diffs.append(jnp.sum(acc[r - 1] - acc[r], axis=0, keepdims=True))
                lanes = pl.ds(pl.multiple_of(first + t * LANES, LANES), LANES)
                out_ref[row, levels, lanes] = jnp.concatenate(diffs, axis=0) * weight_ref[half, levels, cols]

        part_a[...] = parts(0)

        def some_runs(h, carry):
            for u in range(TOGETHER):
                b = TOGETHER * h + u
                now, later = (part_a, part_b) if u % 2 == 0 else (part_b, part_a)
                later[...] = parts(jnp.minimum(b + 1, HALVES * RUNS - 1))
                process(now, b)
            return carry

        lax.fori_loop(0, HALVES * RUNS // TOGETHER, some_runs, 0)
        return carry

    lax.fori_loop(0, ROWS_OF_LAT, run_row, 0)


def radiation(gas, mass, cosine, albedo, order, table, light, tally):
    whole = lambda shape: pl.BlockSpec(shape, lambda: (0,) * len(shape))
    n, width = ROWS_OF_LAT, HALVES * TILE
    return pl.pallas_call(
        rad_kernel,
        out_shape=jax.ShapeDtypeStruct((n, TIERS, width), jnp.float32),
        in_specs=[
            pl.BlockSpec(memory_space=pltpu.SMEM),
            pl.BlockSpec(memory_space=pltpu.HBM),
            pl.BlockSpec(memory_space=pltpu.HBM),
            whole((n, width)), whole((n, width)), whole((1, 256)), whole((TERMS, POINTS)), whole((1, POINTS)),
        ],
        out_specs=whole((n, TIERS, width)),
        scratch_shapes=[
            pltpu.VMEM((RUN * POINTS, 2 * LANES), jnp.bfloat16),
            pltpu.VMEM((HALVES, ROWS, TILE), jnp.float32),
            pltpu.VMEM((HALVES, POINTS, TILE), jnp.float32),
            pltpu.VMEM((HALVES, POINTS, TILE), jnp.float32),
            pltpu.VMEM((HALVES, TIERS, TILE), jnp.float32),
            pltpu.VMEM((RUN * POINTS, TILE), jnp.float32),
            pltpu.VMEM((RUN * POINTS, TILE), jnp.float32),
            pltpu.VMEM((HALVES, ROWS, TILE), jnp.float32),
            pltpu.VMEM((POINTS, 2 * LANES), jnp.bfloat16),
            pltpu.VMEM((POINTS, LANES), jnp.float32),
            pltpu.VMEM((256, LANES), jnp.float32),
            pltpu.VMEM((n, width, TIERS * TERMS), jnp.bfloat16),
            pltpu.VMEM((n, width, TIERS), jnp.bfloat16),
            pltpu.SemaphoreType.DMA((n, HALVES)),
            pltpu.SemaphoreType.DMA((n, HALVES)),
        ],
        compiler_params=pltpu.CompilerParams(vmem_limit_bytes=60 * MIB),
        cost_estimate=pl.CostEstimate(flops=2 * 10 ** 10, bytes_accessed=6 * 10 ** 6, transcendentals=6 * 10 ** 7),
    )(tally, gas, mass, cosine, albedo, order, table, light)


def step(field, west, east, south, north, weights):
    return (
        field
        + weights[0] * (west - field)
        + weights[1] * (east - field)
        + weights[2] * (south - field)
        + weights[3] * (north - field)
    )


def copy_all(copies):
    for copy in copies:
        copy.start()
    for copy in copies:
        copy.wait()


def stacked_copies(sources, lanes, target, target_lanes, sems):
    copies, at = [], 0
    for k, source in enumerate(sources):
        depth = source.shape[0]
        copies.append(pltpu.make_async_copy(
            source.at[:, :, lanes], target.at[at:at + depth, :, target_lanes], sems.at[k]))
        at += depth
    return copies


def rims_kernel(field_ref, zonal_ref, meridional_ref, first_ref, last_ref, sems):
    width = field_ref.shape[2]
    sources = (field_ref, zonal_ref, meridional_ref)
    every = slice(0, HALO)
    copy_all(
        stacked_copies(sources, slice(0, HALO), first_ref, every, sems.at[0])
        + stacked_copies(sources, slice(width - HALO, width), last_ref, every, sems.at[1])
    )


def widened_kernel(field_ref, zonal_ref, meridional_ref, west_ref, east_ref, wide_ref, sems):
    width = field_ref.shape[2]
    copy_all(
        stacked_copies((field_ref, zonal_ref, meridional_ref), slice(0, width), wide_ref,
                       slice(HALO, HALO + width), sems.at[0])
        + stacked_copies((west_ref,), slice(0, HALO), wide_ref, slice(0, HALO), sems.at[1])
        + stacked_copies((east_ref,), slice(0, HALO), wide_ref, slice(HALO + width, HALO + width + HALO), sems.at[2])
    )


def moved(kernel, out_shape, groups, *arrays):
    anywhere = pl.BlockSpec(memory_space=pltpu.HBM)
    return pl.pallas_call(
        kernel,
        out_shape=out_shape,
        in_specs=[anywhere] * len(arrays),
        out_specs=jax.tree.map(lambda shape: anywhere, out_shape),
        scratch_shapes=[pltpu.SemaphoreType.DMA((groups, 3))],
        compiler_params=pltpu.CompilerParams(vmem_limit_bytes=60 * MIB),
    )(*arrays)


def march_kernel(own_ref, south_ref, north_ref, own_weights, south_weights, north_weights, heat_ref, out_ref):
    width = own_ref.shape[2] - 2 * HALO
    rows = {-2: (south_ref, 0), -1: (south_ref, 1), 0: (own_ref, 0), 1: (own_ref, 1), 2: (north_ref, 0), 3: (north_ref, 1)}
    of_row = {-1: (south_weights, 1), 0: (own_weights, 0), 1: (own_weights, 1), 2: (north_weights, 0)}
    middle = slice(HALO, HALO + width)

    def wide(row, levels):
        ref, at = rows[row]
        return ref[levels, at, :]

    def plain(row, levels):
        ref, at = rows[row]
        return ref[levels, at, middle]

    def west_of(cells):
        return pltpu.roll(cells, 1, 1)

    def east_of(cells):
        return pltpu.roll(cells, cells.shape[1] - 1, 1)

    weights = {}
    for row in (-1, 0, 1, 2):
        ref, at = of_row[row]
        lanes = slice(None) if row in (0, 1) else middle
        weights[row] = [ref[k:k + 1, at, lanes] for k in range(4)]
    chunk = 16

    def levels_step(h, carry):
        levels = pl.ds(pl.multiple_of(h * chunk, chunk), chunk)
        first = {row: wide(row, levels) for row in (-1, 0, 1, 2)}
        second = {}
        for row in (0, 1):
            f = first[row]
            second[row] = step(f, west_of(f), east_of(f), first[row - 1], first[row + 1], weights[row])
        for row in (-1, 2):
            f = first[row]
            south = plain(row - 1, levels) if row < 0 else first[row - 1][:, middle]
            north = first[row + 1][:, middle] if row < 0 else plain(row + 1, levels)
            second[row] = step(
                f[:, middle], west_of(f)[:, middle], east_of(f)[:, middle], south, north, weights[row]
            )
        for row in (0, 1):
            f = second[row]
            south = second[row - 1] if row == 0 else second[row - 1][:, middle]
            north = second[row + 1][:, middle] if row == 0 else second[row + 1]
            third = step(
                f[:, middle], west_of(f)[:, middle], east_of(f)[:, middle], south, north,
                [w[:, middle] for w in weights[row]],
            )
            out_ref[levels, row, :] = third + heat_ref[row, levels, :]
        return carry

    lax.fori_loop(0, heat_ref.shape[1] // chunk, levels_step, 0)


def march(own, south, north, heat):
    stripes, reach, width = own.shape[1], own.shape[2], heat.shape[2]
    deep = 32
    cells = pl.BlockSpec((deep, stripes, reach), lambda i: (i, 0, 0))
    weights = pl.BlockSpec((4, stripes, reach), lambda i: (TIERS // 4, 0, 0))
    return pl.pallas_call(
        march_kernel,
        grid=(TIERS // deep,),
        in_specs=[cells] * 3 + [weights] * 3 + [pl.BlockSpec((stripes, deep, width), lambda i: (0, i, 0))],
        out_specs=pl.BlockSpec((deep, stripes, width), lambda i: (i, 0, 0)),
        out_shape=jax.ShapeDtypeStruct((TIERS, stripes, width), jnp.float32),
        compiler_params=pltpu.CompilerParams(vmem_limit_bytes=60 * MIB),
    )(own, south, north, own, south, north, heat)


def shifted(cells, axis, by, closed):
    count = lax.axis_size(axis)
    pairs = [(i, (i + by) % count) for i in range(count) if closed or 0 <= i + by < count]
    return lax.ppermute(cells, axis, pairs)


def per_device(
    thermal_field,
    zonal_weights,
    meridional_weights,
    gas_burden,
    tier_air_weight,
    solar_elevation_factor,
    ground_reflectance,
    extinction_table,
    incoming_irradiance,
    daytime_tile_tally,
    daytime_tile_order,
):
    parts = (thermal_field, zonal_weights, meridional_weights)
    depth, stripes, width = TIERS + 4, thermal_field.shape[1], thermal_field.shape[2]
    rim = jax.ShapeDtypeStruct((depth, stripes, HALO), jnp.float32)
    first, last = moved(rims_kernel, (rim, rim), 2, *parts)
    west = shifted(last, "lon", 1, True)
    east = shifted(first, "lon", -1, True)
    broad = jax.ShapeDtypeStruct((depth, stripes, width + 2 * HALO), jnp.float32)
    own = moved(widened_kernel, broad, 3, *parts, west, east)
    own, gas_burden = lax.optimization_barrier((own, gas_burden))
    south = shifted(own, "lat", 1, False)
    north = shifted(own, "lat", -1, False)
    heat = radiation(
        gas_burden,
        tier_air_weight,
        solar_elevation_factor,
        ground_reflectance,
        daytime_tile_order.reshape(1, -1),
        extinction_table,
        incoming_irradiance.reshape(1, -1),
        daytime_tile_tally,
    )
    return march(own, south, north, heat)


def solution(mesh):
    placed = (
        P(None, "lat", "lon"),
        P(None, "lat", "lon"),
        P(None, "lat", "lon"),
        P("lat", "lon", None),
        P("lat", "lon", None),
        P("lat", "lon"),
        P("lat", "lon"),
        P(),
        P(),
        P("lat", "lon"),
        P("lat", "lon", None),
    )
    return jax.shard_map(
        per_device, mesh=mesh, in_specs=placed, out_specs=P(None, "lat", "lon"), check_vma=False
    )
```

```python
import functools
import math

import jax
import jax.numpy as jnp
from jax import lax
from jax.experimental import pallas as pl
from jax.experimental.pallas import tpu as pltpu
from jax.sharding import PartitionSpec as P

DSTEPS = 2
DIFFUSE = 1.66
LOG2E = math.log2(math.e)
TIERS, TERMS, POINTS, BLOCK = 128, 16, 224, 4
RUN = 8
RUNS = TIERS // RUN
TILE = 256
ROWS = 8
LANES = 128
TOGETHER = 4
HALO = 128
ROWS_OF_LAT, HALVES = 2, 2
MIB = 1024 * 1024
MARCH_MIB = 50


def across(row, rows):
    return jnp.broadcast_to(row, (rows, row.shape[1]))


def halves(values):
    high = values.astype(jnp.bfloat16)
    low = (values - high.astype(jnp.float32)).astype(jnp.bfloat16)
    return jnp.concatenate([high, low], axis=1)


def thirds(values):
    high = values.astype(jnp.bfloat16)
    left = values - high.astype(jnp.float32)
    middle = left.astype(jnp.bfloat16)
    low = (left - middle.astype(jnp.float32)).astype(jnp.bfloat16)
    return high, middle, low


def by_rows(left, right):
    return lax.dot_general(left, right, (((1,), (1,)), ((), ())), preferred_element_type=jnp.float32)


def rad_kernel(row, tally_ref, gas_hbm, mass_hbm, cos_ref, alb_ref, order_ref, table_ref, light_ref, out_ref,
               lhs_ref, slope_ref, down_ref, up_ref, weight_ref, part_a, part_b, net_ref, whole_ref, light_log_ref, listed_ref,
               gas_ref, mass_ref, gas_sem, mass_sem):
    width = 2 * TILE

    def copies(half):
        cols = pl.ds(half * TILE, TILE)
        return (
            pltpu.make_async_copy(gas_hbm.at[row, cols], gas_ref.at[cols], gas_sem.at[half]),
            pltpu.make_async_copy(mass_hbm.at[row, cols], mass_ref.at[cols], mass_sem.at[half]),
        )

    for half in range(HALVES):
        for copy in copies(half):
            copy.start()
    table = table_ref[...] * DIFFUSE
    table = jnp.concatenate([table, jnp.zeros((TERMS, 256 - POINTS), jnp.float32)], axis=1)
    stacked = jnp.concatenate([table] * RUN, axis=0).T[:POINTS]
    whole = halves(stacked * LOG2E)
    term = (lax.broadcasted_iota(jnp.int32, (1, 2 * LANES), 1) & (LANES - 1)) >> 4
    whole_wide = whole.astype(jnp.float32)
    for r in range(1, RUN + 1):
        chosen = jnp.where(term < r, whole_wide, 0.0)
        lhs_ref[(r - 1) * POINTS:r * POINTS, :] = chosen.astype(jnp.bfloat16)
    light = jnp.concatenate([light_ref[...], jnp.ones((1, 256 - POINTS), jnp.float32)], axis=1)
    light = across(jnp.log(light) * LOG2E, LANES).T[:POINTS]
    light_log_ref[...] = light
    whole_ref[...] = whole
    listed = across(order_ref[...].astype(jnp.float32), LANES).T
    rank = lax.broadcasted_iota(jnp.int32, listed.shape, 0)
    listed_ref[...] = jnp.where(rank < tally_ref[0, 0], listed, -1.0)

    def prepare(half):
        first = half * TILE
        cols = slice(first, first + TILE)

        def of_row(ref):
            return ref[:, cols].astype(jnp.float32)[row:row + 1]

        cosine, albedo = of_row(cos_ref), of_row(alb_ref)
        slope = -1.0 / (DIFFUSE * cosine)
        slope_ref[half] = across(slope, ROWS)
        for copy in copies(half):
            copy.wait()
        amount = gas_ref[cols, 0:LANES].astype(jnp.float32)
        for b in range(1, RUNS):
            amount = amount + gas_ref[cols, b * LANES:(b + 1) * LANES].astype(jnp.float32)
        total = None
        for piece in thirds(amount):
            got = by_rows(whole_ref[...], jnp.concatenate([piece, piece], axis=1))
            total = got if total is None else total + got
        light = jnp.concatenate([light_log_ref[...]] * 2, axis=1)
        floor = light + (jnp.log(albedo) * LOG2E) + (slope - 1.0) * total
        down_ref[half] = light
        up_ref[half] = floor
        top = jnp.exp2(light) - jnp.exp2(floor)
        net_ref[half] = jnp.sum(top.reshape(POINTS // ROWS, ROWS, TILE), axis=0)
        eye = (lax.broadcasted_iota(jnp.int32, (LANES, LANES), 0)
               == lax.broadcasted_iota(jnp.int32, (LANES, LANES), 1)).astype(jnp.float32).astype(jnp.bfloat16)
        mass = by_rows(eye, mass_ref[cols, :])
        lit = []
        for t in range(TILE // LANES):
            block = (lax.broadcasted_iota(jnp.int32, (1, LANES), 1) + (row * width + first + t * LANES)) >> 2
            hit = jnp.where(listed_ref[...] == block.astype(jnp.float32), 1.0, 0.0)
            lit.append(jnp.sum(hit, axis=0, keepdims=True))
        lit = jnp.concatenate(lit, axis=1)
        weight_ref[half] = cosine * lit / mass

    for half in range(HALVES):
        prepare(half)

    def place(n):
        half, b = n >> 4, n & (RUNS - 1)
        return half, pl.multiple_of(half * TILE, TILE), b

    def parts(n):
        half, first, b = place(n)
        g = gas_ref[pl.ds(first, TILE), pl.ds(pl.multiple_of(b * LANES, LANES), LANES)]
        return by_rows(lhs_ref[...], jnp.concatenate([g, g], axis=1))

    def process(part_ref, n):
        half, first, b = place(n)
        levels = pl.ds(pl.multiple_of(b * RUN, RUN), RUN)
        for t in range(TILE // LANES):
            cols = slice(t * LANES, (t + 1) * LANES)
            s = slope_ref[half, :, cols]
            acc = [None] * (RUN + 1)
            for q in range(POINTS // ROWS):
                here = slice(q * ROWS, (q + 1) * ROWS)
                down0 = down_ref[half, here, cols]
                up0 = up_ref[half, here, cols]
                for r in range(1, RUN + 1):
                    at = (r - 1) * POINTS + q * ROWS
                    part = part_ref[at:at + ROWS, cols]
                    down = s * part + down0
                    up = part + up0
                    light = jnp.exp2(down)
                    acc[r] = (light if acc[r] is None else acc[r] + light) - jnp.exp2(up)
                down_ref[half, here, cols] = down
                up_ref[half, here, cols] = up
            acc[0] = net_ref[half, :, cols]
            net_ref[half, :, cols] = acc[RUN]
            diffs = []
            for r in range(1, RUN + 1):
                diffs.append(jnp.sum(acc[r - 1] - acc[r], axis=0, keepdims=True))
            lanes = pl.ds(pl.multiple_of(first + t * LANES, LANES), LANES)
            out_ref[levels, lanes] = jnp.concatenate(diffs, axis=0) * weight_ref[half, levels, cols]

    part_a[...] = parts(0)

    def some_runs(h, carry):
        for u in range(TOGETHER):
            b = TOGETHER * h + u
            now, later = (part_a, part_b) if u % 2 == 0 else (part_b, part_a)
            later[...] = parts(jnp.minimum(b + 1, HALVES * RUNS - 1))
            process(now, b)
        return carry

    lax.fori_loop(0, HALVES * RUNS // TOGETHER, some_runs, 0)


def radiation(gas, mass, cosine, albedo, order, table, light, tally, row):
    whole = lambda shape: pl.BlockSpec(shape, lambda: (0,) * len(shape))
    n, width = ROWS_OF_LAT, HALVES * TILE
    return pl.pallas_call(
        functools.partial(rad_kernel, row),
        out_shape=jax.ShapeDtypeStruct((TIERS, width), jnp.float32),
        in_specs=[
            pl.BlockSpec(memory_space=pltpu.SMEM),
            pl.BlockSpec(memory_space=pltpu.HBM),
            pl.BlockSpec(memory_space=pltpu.HBM),
            whole((n, width)), whole((n, width)), whole((1, 256)), whole((TERMS, POINTS)), whole((1, POINTS)),
        ],
        out_specs=whole((TIERS, width)),
        scratch_shapes=[
            pltpu.VMEM((RUN * POINTS, 2 * LANES), jnp.bfloat16),
            pltpu.VMEM((HALVES, ROWS, TILE), jnp.float32),
            pltpu.VMEM((HALVES, POINTS, TILE), jnp.float32),
            pltpu.VMEM((HALVES, POINTS, TILE), jnp.float32),
            pltpu.VMEM((HALVES, TIERS, TILE), jnp.float32),
            pltpu.VMEM((RUN * POINTS, TILE), jnp.float32),
            pltpu.VMEM((RUN * POINTS, TILE), jnp.float32),
            pltpu.VMEM((HALVES, ROWS, TILE), jnp.float32),
            pltpu.VMEM((POINTS, 2 * LANES), jnp.bfloat16),
            pltpu.VMEM((POINTS, LANES), jnp.float32),
            pltpu.VMEM((256, LANES), jnp.float32),
            pltpu.VMEM((width, TIERS * TERMS), jnp.bfloat16),
            pltpu.VMEM((width, TIERS), jnp.bfloat16),
            pltpu.SemaphoreType.DMA((HALVES,)),
            pltpu.SemaphoreType.DMA((HALVES,)),
        ],
        compiler_params=pltpu.CompilerParams(vmem_limit_bytes=60 * MIB),
        cost_estimate=pl.CostEstimate(flops=2 * 10 ** 10, bytes_accessed=6 * 10 ** 6, transcendentals=6 * 10 ** 7),
    )(tally, gas, mass, cosine, albedo, order, table, light)


def step(field, west, east, south, north, weights):
    return (
        field
        + weights[0] * (west - field)
        + weights[1] * (east - field)
        + weights[2] * (south - field)
        + weights[3] * (north - field)
    )


DEPTH = TIERS + 8


def gathered_kernel(field_ref, zonal_ref, meridional_ref, own_ref):
    for row in range(ROWS_OF_LAT):
        own_ref[row, 0:TIERS, :] = field_ref[:, row, :]
        weights = [ref[k:k + 1, row, :] for ref in (zonal_ref, meridional_ref) for k in range(2)]
        own_ref[row, TIERS:DEPTH, :] = jnp.concatenate(weights + weights, axis=0)


def gathered(field, zonal, meridional):
    return pl.pallas_call(
        gathered_kernel,
        out_shape=jax.ShapeDtypeStruct((ROWS_OF_LAT, DEPTH, field.shape[2]), jnp.float32),
        compiler_params=pltpu.CompilerParams(vmem_limit_bytes=60 * MIB),
    )(field, zonal, meridional)


def march_kernel(own_ref, south_ref, north_ref, west_ref, east_ref, heat0_ref, heat1_ref, out_ref):
    width = own_ref.shape[2]
    rows = {-2: (south_ref, 0), -1: (south_ref, 1), 0: (own_ref, 0), 1: (own_ref, 1), 2: (north_ref, 0), 3: (north_ref, 1)}
    middle = slice(HALO, HALO + width)

    def plain(row, levels):
        ref, at = rows[row]
        return ref[at, levels, :]

    def wide(row, levels):
        return jnp.concatenate(
            [west_ref[row + 1, levels, :], plain(row, levels), east_ref[row + 1, levels, :]], axis=1
        )

    def west_of(cells):
        return pltpu.roll(cells, 1, 1)

    def east_of(cells):
        return pltpu.roll(cells, cells.shape[1] - 1, 1)

    weights = {}
    for row in (-1, 0, 1, 2):
        load = wide if row in (0, 1) else plain
        weights[row] = [load(row, slice(TIERS + k, TIERS + k + 1)) for k in range(4)]
    chunk = 16

    def levels_step(h, carry):
        levels = pl.ds(pl.multiple_of(h * chunk, chunk), chunk)
        first = {row: wide(row, levels) for row in (-1, 0, 1, 2)}
        second = {}
        for row in (0, 1):
            f = first[row]
            second[row] = step(f, west_of(f), east_of(f), first[row - 1], first[row + 1], weights[row])
        for row in (-1, 2):
            f = first[row]
            south = plain(row - 1, levels) if row < 0 else first[row - 1][:, middle]
            north = first[row + 1][:, middle] if row < 0 else plain(row + 1, levels)
            second[row] = step(
                f[:, middle], west_of(f)[:, middle], east_of(f)[:, middle], south, north, weights[row]
            )
        for row, heat_ref in ((0, heat0_ref), (1, heat1_ref)):
            f = second[row]
            south = second[row - 1] if row == 0 else second[row - 1][:, middle]
            north = second[row + 1][:, middle] if row == 0 else second[row + 1]
            third = step(
                f[:, middle], west_of(f)[:, middle], east_of(f)[:, middle], south, north,
                [w[:, middle] for w in weights[row]],
            )
            out_ref[levels, row, :] = third + heat_ref[levels, :]
        return carry

    lax.fori_loop(0, TIERS // chunk, levels_step, 0)


def march(own, south, north, west, east, heat0, heat1):
    return pl.pallas_call(
        march_kernel,
        out_shape=jax.ShapeDtypeStruct((TIERS, ROWS_OF_LAT, own.shape[2]), jnp.float32),
        compiler_params=pltpu.CompilerParams(vmem_limit_bytes=MARCH_MIB * MIB),
    )(own, south, north, west, east, heat0, heat1)


def shifted(cells, axis, by, closed):
    count = lax.axis_size(axis)
    pairs = [(i, (i + by) % count) for i in range(count) if closed or 0 <= i + by < count]
    return lax.ppermute(cells, axis, pairs)


def per_device(
    thermal_field,
    zonal_weights,
    meridional_weights,
    gas_burden,
    tier_air_weight,
    solar_elevation_factor,
    ground_reflectance,
    extinction_table,
    incoming_irradiance,
    daytime_tile_tally,
    daytime_tile_order,
):
    def heating(row, gas):
        return radiation(
            gas,
            tier_air_weight,
            solar_elevation_factor,
            ground_reflectance,
            daytime_tile_order.reshape(1, -1),
            extinction_table,
            incoming_irradiance.reshape(1, -1),
            daytime_tile_tally,
            row,
        )

    own = gathered(thermal_field, zonal_weights, meridional_weights)
    south = shifted(own, "lat", 1, False)
    north = shifted(own, "lat", -1, False)
    heat0 = heating(0, gas_burden)
    south, north, heat0 = lax.optimization_barrier((south, north, heat0))
    near = jnp.concatenate([south[1:], own, north[:1]], axis=0)
    last, first = near[:, :, -HALO:], near[:, :, :HALO]
    gas_burden, last, first = lax.optimization_barrier((gas_burden, last, first))
    west = shifted(last, "lon", 1, True)
    east = shifted(first, "lon", -1, True)
    heat1 = heating(1, gas_burden)
    return march(own, south, north, west, east, heat0, heat1)


def solution(mesh):
    placed = (
        P(None, "lat", "lon"),
        P(None, "lat", "lon"),
        P(None, "lat", "lon"),
        P("lat", "lon", None),
        P("lat", "lon", None),
        P("lat", "lon"),
        P("lat", "lon"),
        P(),
        P(),
        P("lat", "lon"),
        P("lat", "lon", None),
    )
    return jax.shard_map(
        per_device, mesh=mesh, in_specs=placed, out_specs=P(None, "lat", "lon"), check_vma=False
    )
```

```python
import functools
import math

import jax
import jax.numpy as jnp
from jax import lax
from jax.experimental import pallas as pl
from jax.experimental.pallas import tpu as pltpu
from jax.sharding import PartitionSpec as P

DSTEPS = 2
DIFFUSE = 1.66
LOG2E = math.log2(math.e)
TIERS, TERMS, POINTS, BLOCK = 128, 16, 224, 4
RUN = 8
RUNS = TIERS // RUN
TILE = 256
ROWS = 8
LANES = 128
TOGETHER = 8
HALO = 128
ROWS_OF_LAT, HALVES = 2, 2
MIB = 1024 * 1024
MARCH_MIB = 50


def across(row, rows):
    return jnp.broadcast_to(row, (rows, row.shape[1]))


def halves(values):
    high = values.astype(jnp.bfloat16)
    low = (values - high.astype(jnp.float32)).astype(jnp.bfloat16)
    return jnp.concatenate([high, low], axis=1)


def thirds(values):
    high = values.astype(jnp.bfloat16)
    left = values - high.astype(jnp.float32)
    middle = left.astype(jnp.bfloat16)
    low = (left - middle.astype(jnp.float32)).astype(jnp.bfloat16)
    return high, middle, low


def by_rows(left, right):
    return lax.dot_general(left, right, (((1,), (1,)), ((), ())), preferred_element_type=jnp.float32)


def rad_kernel(row, tally_ref, gas_hbm, mass_hbm, cos_hbm, alb_hbm, order_hbm, table_hbm, light_hbm, out_ref,
               lhs_ref, slope_ref, down_ref, up_ref, weight_ref, part_a, part_b, net_ref, whole_ref, light_log_ref, listed_ref,
               gas_ref, mass_ref, gas_sem, mass_sem,
               cos_ref, alb_ref, order_ref, table_ref, light_ref, small_sem):
    width = 2 * TILE

    def copies(half):
        cols = pl.ds(half * TILE, TILE)
        return (
            pltpu.make_async_copy(gas_hbm.at[row, cols], gas_ref.at[cols], gas_sem.at[half]),
            pltpu.make_async_copy(mass_hbm.at[row, cols], mass_ref.at[cols], mass_sem.at[half]),
        )

    small = [
        pltpu.make_async_copy(source, target, small_sem.at[k])
        for k, (source, target) in enumerate((
            (table_hbm, table_ref), (light_hbm, light_ref), (order_hbm, order_ref),
            (cos_hbm, cos_ref), (alb_hbm, alb_ref),
        ))
    ]
    for copy in small:
        copy.start()
    for half in range(HALVES):
        for copy in copies(half):
            copy.start()
    for copy in small:
        copy.wait()
    table = table_ref[...] * DIFFUSE
    table = jnp.concatenate([table, jnp.zeros((TERMS, 256 - POINTS), jnp.float32)], axis=1)
    stacked = jnp.concatenate([table] * RUN, axis=0).T[:POINTS]
    whole = halves(stacked * LOG2E)
    term = (lax.broadcasted_iota(jnp.int32, (1, 2 * LANES), 1) & (LANES - 1)) >> 4
    whole_wide = whole.astype(jnp.float32)
    for r in range(1, RUN + 1):
        chosen = jnp.where(term < r, whole_wide, 0.0)
        lhs_ref[(r - 1) * POINTS:r * POINTS, :] = chosen.astype(jnp.bfloat16)
    light = jnp.concatenate([light_ref[...], jnp.ones((1, 256 - POINTS), jnp.float32)], axis=1)
    light = across(jnp.log(light) * LOG2E, LANES).T[:POINTS]
    light_log_ref[...] = light
    whole_ref[...] = whole
    listed = across(order_ref[...].astype(jnp.float32), LANES).T
    rank = lax.broadcasted_iota(jnp.int32, listed.shape, 0)
    listed_ref[...] = jnp.where(rank < tally_ref[0, 0], listed, -1.0)

    def prepare(half):
        first = half * TILE
        cols = slice(first, first + TILE)

        def of_row(ref):
            return ref[:, cols].astype(jnp.float32)[row:row + 1]

        cosine, albedo = of_row(cos_ref), of_row(alb_ref)
        slope = -1.0 / (DIFFUSE * cosine)
        slope_ref[half] = across(slope, ROWS)
        for copy in copies(half):
            copy.wait()
        amount = gas_ref[cols, 0:LANES].astype(jnp.float32)
        for b in range(1, RUNS):
            amount = amount + gas_ref[cols, b * LANES:(b + 1) * LANES].astype(jnp.float32)
        total = None
        for piece in thirds(amount):
            got = by_rows(whole_ref[...], jnp.concatenate([piece, piece], axis=1))
            total = got if total is None else total + got
        light = jnp.concatenate([light_log_ref[...]] * 2, axis=1)
        floor = light + (jnp.log(albedo) * LOG2E) + (slope - 1.0) * total
        down_ref[half] = light
        up_ref[half] = floor
        top = jnp.exp2(light) - jnp.exp2(floor)
        net_ref[half] = jnp.sum(top.reshape(POINTS // ROWS, ROWS, TILE), axis=0)
        eye = (lax.broadcasted_iota(jnp.int32, (LANES, LANES), 0)
               == lax.broadcasted_iota(jnp.int32, (LANES, LANES), 1)).astype(jnp.float32).astype(jnp.bfloat16)
        mass = by_rows(eye, mass_ref[cols, :])
        lit = []
        for t in range(TILE // LANES):
            block = (lax.broadcasted_iota(jnp.int32, (1, LANES), 1) + (row * width + first + t * LANES)) >> 2
            hit = jnp.where(listed_ref[...] == block.astype(jnp.float32), 1.0, 0.0)
            lit.append(jnp.sum(hit, axis=0, keepdims=True))
        lit = jnp.concatenate(lit, axis=1)
        weight_ref[half] = cosine * lit / mass

    for half in range(HALVES):
        prepare(half)

    def place(n):
        half, b = n >> 4, n & (RUNS - 1)
        return half, pl.multiple_of(half * TILE, TILE), b

    def parts(n):
        half, first, b = place(n)
        g = gas_ref[pl.ds(first, TILE), pl.ds(pl.multiple_of(b * LANES, LANES), LANES)]
        return by_rows(lhs_ref[...], jnp.concatenate([g, g], axis=1))

    def process(part_ref, n):
        half, first, b = place(n)
        levels = pl.ds(pl.multiple_of(b * RUN, RUN), RUN)
        for t in range(TILE // LANES):
            cols = slice(t * LANES, (t + 1) * LANES)
            s = slope_ref[half, :, cols]
            acc = [None] * (RUN + 1)
            for q in range(POINTS // ROWS):
                here = slice(q * ROWS, (q + 1) * ROWS)
                down0 = down_ref[half, here, cols]
                up0 = up_ref[half, here, cols]
                for r in range(1, RUN + 1):
                    at = (r - 1) * POINTS + q * ROWS
                    part = part_ref[at:at + ROWS, cols]
                    down = s * part + down0
                    up = part + up0
                    light = jnp.exp2(down)
                    acc[r] = (light if acc[r] is None else acc[r] + light) - jnp.exp2(up)
                down_ref[half, here, cols] = down
                up_ref[half, here, cols] = up
            acc[0] = net_ref[half, :, cols]
            net_ref[half, :, cols] = acc[RUN]
            diffs = []
            for r in range(1, RUN + 1):
                diffs.append(jnp.sum(acc[r - 1] - acc[r], axis=0, keepdims=True))
            lanes = pl.ds(pl.multiple_of(first + t * LANES, LANES), LANES)
            out_ref[levels, lanes] = jnp.concatenate(diffs, axis=0) * weight_ref[half, levels, cols]

    part_a[...] = parts(0)

    def some_runs(h, carry):
        for u in range(TOGETHER):
            b = TOGETHER * h + u
            now, later = (part_a, part_b) if u % 2 == 0 else (part_b, part_a)
            later[...] = parts(jnp.minimum(b + 1, HALVES * RUNS - 1))
            process(now, b)
        return carry

    lax.fori_loop(0, HALVES * RUNS // TOGETHER, some_runs, 0)


def radiation(gas, mass, cosine, albedo, order, table, light, tally, row):
    whole = lambda shape: pl.BlockSpec(shape, lambda: (0,) * len(shape))
    n, width = ROWS_OF_LAT, HALVES * TILE
    return pl.pallas_call(
        functools.partial(rad_kernel, row),
        out_shape=jax.ShapeDtypeStruct((TIERS, width), jnp.float32),
        in_specs=[
            pl.BlockSpec(memory_space=pltpu.SMEM),
            pl.BlockSpec(memory_space=pltpu.HBM),
            pl.BlockSpec(memory_space=pltpu.HBM),
            *[pl.BlockSpec(memory_space=pltpu.HBM)] * 5,
        ],
        out_specs=whole((TIERS, width)),
        scratch_shapes=[
            pltpu.VMEM((RUN * POINTS, 2 * LANES), jnp.bfloat16),
            pltpu.VMEM((HALVES, ROWS, TILE), jnp.float32),
            pltpu.VMEM((HALVES, POINTS, TILE), jnp.float32),
            pltpu.VMEM((HALVES, POINTS, TILE), jnp.float32),
            pltpu.VMEM((HALVES, TIERS, TILE), jnp.float32),
            pltpu.VMEM((RUN * POINTS, TILE), jnp.float32),
            pltpu.VMEM((RUN * POINTS, TILE), jnp.float32),
            pltpu.VMEM((HALVES, ROWS, TILE), jnp.float32),
            pltpu.VMEM((POINTS, 2 * LANES), jnp.bfloat16),
            pltpu.VMEM((POINTS, LANES), jnp.float32),
            pltpu.VMEM((256, LANES), jnp.float32),
            pltpu.VMEM((width, TIERS * TERMS), jnp.bfloat16),
            pltpu.VMEM((width, TIERS), jnp.bfloat16),
            pltpu.SemaphoreType.DMA((HALVES,)),
            pltpu.SemaphoreType.DMA((HALVES,)),
            pltpu.VMEM((n, width), jnp.bfloat16),
            pltpu.VMEM((n, width), jnp.bfloat16),
            pltpu.VMEM((1, 256), jnp.int32),
            pltpu.VMEM((TERMS, POINTS), jnp.float32),
            pltpu.VMEM((1, POINTS), jnp.float32),
            pltpu.SemaphoreType.DMA((5,)),
        ],
        compiler_params=pltpu.CompilerParams(vmem_limit_bytes=60 * MIB),
        cost_estimate=pl.CostEstimate(flops=2 * 10 ** 10, bytes_accessed=6 * 10 ** 6, transcendentals=6 * 10 ** 7),
    )(tally, gas, mass, cosine, albedo, order, table, light)


def step(field, west, east, south, north, weights):
    return (
        field
        + weights[0] * (west - field)
        + weights[1] * (east - field)
        + weights[2] * (south - field)
        + weights[3] * (north - field)
    )


DEPTH = TIERS + 8


def gathered_kernel(field_ref, zonal_ref, meridional_ref, own_ref):
    for row in range(ROWS_OF_LAT):
        own_ref[row, 0:TIERS, :] = field_ref[:, row, :]
        weights = [ref[k:k + 1, row, :] for ref in (zonal_ref, meridional_ref) for k in range(2)]
        own_ref[row, TIERS:DEPTH, :] = jnp.concatenate(weights + weights, axis=0)


def gathered(field, zonal, meridional):
    return pl.pallas_call(
        gathered_kernel,
        out_shape=jax.ShapeDtypeStruct((ROWS_OF_LAT, DEPTH, field.shape[2]), jnp.float32),
        compiler_params=pltpu.CompilerParams(vmem_limit_bytes=60 * MIB),
    )(field, zonal, meridional)


def march_kernel(own_ref, south_ref, north_ref, west_ref, east_ref, heat0_ref, heat1_ref, out_ref):
    width = own_ref.shape[2]
    rows = {-2: (south_ref, 0), -1: (south_ref, 1), 0: (own_ref, 0), 1: (own_ref, 1), 2: (north_ref, 0), 3: (north_ref, 1)}
    middle = slice(HALO, HALO + width)

    def plain(row, levels):
        ref, at = rows[row]
        return ref[at, levels, :]

    def wide(row, levels):
        return jnp.concatenate(
            [west_ref[row + 1, levels, :], plain(row, levels), east_ref[row + 1, levels, :]], axis=1
        )

    def west_of(cells):
        return pltpu.roll(cells, 1, 1)

    def east_of(cells):
        return pltpu.roll(cells, cells.shape[1] - 1, 1)

    weights = {}
    for row in (-1, 0, 1, 2):
        load = wide if row in (0, 1) else plain
        weights[row] = [load(row, slice(TIERS + k, TIERS + k + 1)) for k in range(4)]
    chunk = 16

    def levels_step(h, carry):
        levels = pl.ds(pl.multiple_of(h * chunk, chunk), chunk)
        first = {row: wide(row, levels) for row in (-1, 0, 1, 2)}
        second = {}
        for row in (0, 1):
            f = first[row]
            second[row] = step(f, west_of(f), east_of(f), first[row - 1], first[row + 1], weights[row])
        for row in (-1, 2):
            f = first[row]
            south = plain(row - 1, levels) if row < 0 else first[row - 1][:, middle]
            north = first[row + 1][:, middle] if row < 0 else plain(row + 1, levels)
            second[row] = step(
                f[:, middle], west_of(f)[:, middle], east_of(f)[:, middle], south, north, weights[row]
            )
        for row, heat_ref in ((0, heat0_ref), (1, heat1_ref)):
            f = second[row]
            south = second[row - 1] if row == 0 else second[row - 1][:, middle]
            north = second[row + 1][:, middle] if row == 0 else second[row + 1]
            third = step(
                f[:, middle], west_of(f)[:, middle], east_of(f)[:, middle], south, north,
                [w[:, middle] for w in weights[row]],
            )
            out_ref[levels, row, :] = third + heat_ref[levels, :]
        return carry

    lax.fori_loop(0, TIERS // chunk, levels_step, 0)


def march(own, south, north, west, east, heat0, heat1):
    return pl.pallas_call(
        march_kernel,
        out_shape=jax.ShapeDtypeStruct((TIERS, ROWS_OF_LAT, own.shape[2]), jnp.float32),
        compiler_params=pltpu.CompilerParams(vmem_limit_bytes=MARCH_MIB * MIB),
    )(own, south, north, west, east, heat0, heat1)


def shifted(cells, axis, by, closed):
    count = lax.axis_size(axis)
    pairs = [(i, (i + by) % count) for i in range(count) if closed or 0 <= i + by < count]
    return lax.ppermute(cells, axis, pairs)


def per_device(
    thermal_field,
    zonal_weights,
    meridional_weights,
    gas_burden,
    tier_air_weight,
    solar_elevation_factor,
    ground_reflectance,
    extinction_table,
    incoming_irradiance,
    daytime_tile_tally,
    daytime_tile_order,
):
    def heating(row, gas):
        return radiation(
            gas,
            tier_air_weight,
            solar_elevation_factor,
            ground_reflectance,
            daytime_tile_order.reshape(1, -1),
            extinction_table,
            incoming_irradiance.reshape(1, -1),
            daytime_tile_tally,
            row,
        )

    own = gathered(thermal_field, zonal_weights, meridional_weights)
    south = shifted(own, "lat", 1, False)
    north = shifted(own, "lat", -1, False)
    heat0 = heating(0, gas_burden)
    south, north, heat0 = lax.optimization_barrier((south, north, heat0))
    near = jnp.concatenate([south[1:], own, north[:1]], axis=0)
    last, first = near[:, :, -HALO:], near[:, :, :HALO]
    gas_burden, last, first = lax.optimization_barrier((gas_burden, last, first))
    west = shifted(last, "lon", 1, True)
    east = shifted(first, "lon", -1, True)
    heat1 = heating(1, gas_burden)
    return march(own, south, north, west, east, heat0, heat1)


def solution(mesh):
    placed = (
        P(None, "lat", "lon"),
        P(None, "lat", "lon"),
        P(None, "lat", "lon"),
        P("lat", "lon", None),
        P("lat", "lon", None),
        P("lat", "lon"),
        P("lat", "lon"),
        P(),
        P(),
        P("lat", "lon"),
        P("lat", "lon", None),
    )
    return jax.shard_map(
        per_device, mesh=mesh, in_specs=placed, out_specs=P(None, "lat", "lon"), check_vma=False
    )
```
